256 devices in a mesh: replica: 8 (over z_lo, y), fsdp: 32 (over x, z_hi, core).
Axes of the slice: x: 4, y: 4, z: 8 (z_hi: 4, z_lo: 2; z = z_hi * 2 + z_lo), core: 2. Of those that a mesh axis runs over, the one named last changes fastest.
Arguments:
- acts: bfloat16 [8, 16384, 8192], P('replica', 'fsdp'), may hold values from -6 to 6
- doc_ids: int32 [8, 16384], P('replica', 'fsdp'), may hold values from 0 to 7, never falling along the last dimension, each value on 1 to 8192 neighbouring positions
- target: bfloat16 [8, 16384, 512], P('replica', 'fsdp'), may hold values from -6 to 6
- inner_weight: float32 [8, 8192, 512], P('replica', 'fsdp'), may hold values from -6 to 6
- adam_first: float32 [8, 8192, 512], P('replica', 'fsdp'), may hold values from -4 to 4
- adam_second: float32 [8, 8192, 512], P('replica', 'fsdp'), may hold values from 0.25 to 4
- outer_weight: float32 [8192, 512], P('fsdp'), may hold values from -6 to 6
- outer_moment: float32 [8192, 512], P('fsdp'), may hold values from -4 to 4
- fragment: int32 [1], replicated, may hold values from 0 to 3
Outputs:
- inner_out: float32 [8, 8192, 512], P('replica', 'fsdp')
- first_out: float32 [8, 8192, 512], P('replica', 'fsdp')
- second_out: float32 [8, 8192, 512], P('replica', 'fsdp')
- outer_out: float32 [8192, 512], P('fsdp')
- moment_out: float32 [8192, 512], P('fsdp')
The draws below stay inside these ranges and needn't reach their ends.
Inputs may be any that keep to these rules, and one draw needn't show every extreme that they name: Within each group doc_ids never falls, every number of 0 to 7 occurs, each document holds at most 8192 tokens and one exactly 8192.
All inputs are finite; a program needn't handle non-finite values.
Results may differ from the reference program's by a relative error of at most 0.0033.
Values may be sent and summed in bfloat16 or wider, within the bound.
No kernel may reach another device: no remote copies, remote signals or barrier semaphores. Data moves between devices by JAX's collectives and lax.ppermute only.
A program may use at most 128 MiB of HBM per device.

```python
import math
import jax
import jax.numpy as jnp
import numpy as np
from jax import lax

D = 8192
HEAD = 128
KW = 512
FRAGS = 4
DOCS = 8
TOKENS = 16384
MOST = 8192
GROUPS = 8
N_REPLICA = 8


def block_scale(rng, dims, split, low, largest):
    def one(position, shards_of):
        heights = jax.random.uniform(jax.random.fold_in(jax.random.fold_in(rng, 6), position), (shards_of,), jnp.float32, low / len(split), largest / len(split))
        return jnp.repeat(jnp.exp(heights), dims[position] // shards_of).reshape((-1,) + (1,) * (len(dims) - position - 1))

    loudness = one(*split[0])
    for cut in split[1:]:
        loudness = loudness * one(*cut)
    return loudness


def split_up(count, total, bound, lean):
    loads = [(1 << 20) // math.isqrt(grade ** lean) + 1 for grade in range(2, count + 1)]
    surplus, holding = total - bound - (count - 1), [1] * (count - 1)
    while surplus > 0:
        candidates = [i for i in range(count - 1) if holding[i] < bound]
        whole, budget = sum([loads[i] for i in candidates]), surplus
        for i in candidates:
            addition = min(bound - holding[i], max(1, budget * loads[i] // whole), surplus)
            holding[i] = holding[i] + addition
            surplus = surplus - addition
    return np.array([bound] + holding)


def ragged(key, amount, total, reach, lean):
    if amount == 2:
        one = jax.random.randint(key, (), max(1, total - reach), min(reach, total - 1) + 1)
        return jnp.stack([one, total - one])
    lengths = jnp.asarray(split_up(amount, total, reach, lean), jnp.int32)
    pairs = (amount - 1) // 2
    donor, sink = lengths[1:1 + 2 * pairs:2], lengths[2:2 + 2 * pairs:2]
    room = jnp.minimum(donor - 1, reach - sink)
    shifted = jax.random.randint(jax.random.fold_in(key, 1), (pairs,), 0, 1 << 20) % (room + 1)
    lengths = lengths.at[1:1 + 2 * pairs:2].set(donor - shifted).at[2:2 + 2 * pairs:2].set(sink + shifted)
    return lengths[jax.random.permutation(jax.random.fold_in(key, 2), amount)]


def noise(rng, extent, spread, reach, pieces=(), kind=jnp.bfloat16):
    entries = jax.random.normal(rng, extent, jnp.float32) * spread
    if len(pieces) > 0:
        entries = block_scale(rng, extent, pieces, -0.22, 0.18) * entries
    return jnp.clip(entries, min=-reach, max=reach).astype(kind)


def setup_inputs(seed: int = 0) -> dict:
    seeds = jax.random.split(jax.random.key(seed), 10)
    acts = noise(seeds[0], (GROUPS, TOKENS, D), 1.0, 6.0, ((0, 8), (1, 32)))
    doc_ids = jax.vmap(lambda own: jnp.searchsorted(jnp.cumsum(ragged(own, DOCS, TOKENS, MOST, 1)), jnp.arange(TOKENS), side="right"))(jax.random.split(seeds[1], GROUPS)).reshape((GROUPS, TOKENS)).astype(jnp.int32)
    target = noise(seeds[2], (GROUPS, TOKENS, KW), 1.0, 6.0, ((0, 8), (1, 32)))
    inner_weight = noise(seeds[3], (GROUPS, D, KW), 1.0, 6.0, ((0, 8), (1, 32)), jnp.float32)
    adam_first = noise(seeds[4], (GROUPS, D, KW), 0.5, 4.0, ((0, 8), (1, 32)), jnp.float32)
    adam_second = jnp.clip(jnp.exp(math.log(4.0) - 2.7725887 * jax.random.uniform(seeds[5], (GROUPS, D, KW), jnp.float32) ** block_scale(seeds[5], (GROUPS, D, KW), ((0, 8), (1, 32)), -0.2, 0.2)), 0.25, 4.0)
    outer_weight = noise(seeds[6], (D, KW), 1.0, 6.0, ((0, 32),), jnp.float32)
    outer_moment = noise(seeds[7], (D, KW), 0.5, 4.0, ((0, 32),), jnp.float32)
    fragment = jax.random.randint(seeds[8], (1,), 0, FRAGS).astype(jnp.int32)
    return {"acts": acts, "doc_ids": doc_ids, "target": target, "inner_weight": inner_weight, "adam_first": adam_first, "adam_second": adam_second, "outer_weight": outer_weight, "outer_moment": outer_moment, "fragment": fragment}


theta_base = 500000.0
first_fix = 0.9999734386011124
second_fix = 0.9940794707796672

def rotary_tables(positions):
    half = HEAD // 2
    index = jnp.arange(half, dtype=jnp.float32)
    freqs = jnp.exp(index * jnp.float32(-2.0 * math.log(theta_base) / HEAD))
    angles = positions.astype(jnp.float32)[:, None] * freqs[None, :]
    return (jnp.cos(angles), jnp.sin(angles))

def rotate(keys, cosine, sine, sign):
    count = keys.shape[0]
    heads = keys.reshape(count, -1, 2, HEAD // 2)
    first = heads[:, :, 0]
    second = heads[:, :, 1]
    cosc = cosine[:, None, :]
    sinc = sign * sine[:, None, :]
    turned = jnp.stack([first * cosc - second * sinc, second * cosc + first * sinc], axis=2)
    return turned.reshape(count, -1)

def group_step(items):
    acts, ids, target, weight, first, second = items
    starts = lax.optimization_barrier(jnp.sum((ids[None, :] < ids[:, None]).astype(jnp.int32), axis=1)).astype(jnp.int32)
    positions = jnp.arange(ids.shape[0], dtype=jnp.int32) - starts
    cosine, sine = rotary_tables(positions)
    keys = jnp.dot(acts, weight.astype(jnp.bfloat16), preferred_element_type=jnp.float32) * D ** (-0.5)
    rotated = rotate(keys, cosine, sine, 1.0)
    back = (rotate(rotated - target.astype(jnp.float32), cosine, sine, -1.0) * TOKENS ** (-0.5)).astype(jnp.bfloat16)
    grad = lax.dot_general(acts, back, (((0,), (0,)), ((), ())), preferred_element_type=jnp.float32)
    first_new = 0.9 * first + 0.1 * grad
    second_new = 0.95 * second + 0.05 * grad * grad
    update = first_new / first_fix / (jnp.sqrt(second_new / second_fix) + 1e-08)
    stepped = weight - 0.02 * (update + 0.1 * weight)
    return (stepped, first_new, second_new)

def reference(acts, doc_ids, target, inner_weight, adam_first, adam_second, outer_weight, outer_moment, fragment):
    stepped, first_out, second_out = lax.map(group_step, (acts, doc_ids, target, inner_weight, adam_first, adam_second))
    cols = KW // FRAGS
    start = (fragment[0] * cols).astype(jnp.int32)
    outer_part = lax.dynamic_slice_in_dim(outer_weight, start, cols, 1)
    moment_part = lax.dynamic_slice_in_dim(outer_moment, start, cols, 1)
    inner_part = lax.dynamic_slice_in_dim(inner_weight, start, cols, 2)
    mean_delta = lax.optimization_barrier(jnp.sum(outer_part[None] - inner_part, axis=0)) / N_REPLICA
    moment_new = 0.9 * moment_part + mean_delta
    outer_new = outer_part - 0.7 * (mean_delta + 0.9 * moment_new)
    blended = 0.5 * lax.dynamic_slice_in_dim(stepped, start, cols, 2) + 0.5 * outer_new[None]
    inner_out = lax.dynamic_update_slice_in_dim(stepped, blended, start, 2)
    outer_out = lax.dynamic_update_slice_in_dim(outer_weight, outer_new, start, 1)
    moment_out = lax.dynamic_update_slice_in_dim(outer_moment, moment_new, start, 1)
    return (inner_out, first_out, second_out, outer_out, moment_out)
```

```python
import math

import jax
import jax.numpy as jnp
from jax import lax
from jax.experimental import pallas as pl
from jax.experimental.pallas import tpu as pltpu
from jax.sharding import PartitionSpec as P

D = 8192
HEAD = 128
FRAGS = 4
DOCS = 8

theta_base = 500000.0
first_fix = 0.9999734386011124
second_fix = 0.9940794707796672

f32 = jnp.float32
bf16 = jnp.bfloat16
VM = pltpu.VMEM
LIMIT = 16 * 1024 * 1024
NOTE = 16
NOWHERE = 128 * 255
NT = (((1,), (1,)), ((), ()))
SCALARS = pl.BlockSpec(memory_space=pltpu.SMEM)

NX, NZ = 4, 4
TORUS = [(x, z, c) for x in range(NX) for z in range(NZ) for c in range(2)]


def place(x, z, c):
    return ((x % NX) * NZ + z % NZ) * 2 + c


def pairs(target):
    return [(place(*at), place(*target(*at))) for at in TORUS]


def way(c):
    return 1 - 2 * c


FROM_X = pairs(lambda x, z, c: (x - way(c), z, c))
FROM_Z = pairs(lambda x, z, c: (x, z - way(c), c))
TO_X = pairs(lambda x, z, c: (x + way(c), z, c))
TO_Z = pairs(lambda x, z, c: (x, z + way(c), c))
SIBLING = pairs(lambda x, z, c: (x, z, 1 - c))


def move(value, table):
    return lax.ppermute(value, "fsdp", table)


def after(value, *others):
    return lax.optimization_barrier((value,) + others)[0]


def params(limit=LIMIT):
    return pltpu.CompilerParams(vmem_limit_bytes=limit)


def cost(flops, moved):
    return pl.CostEstimate(flops=flops, bytes_accessed=moved, transcendentals=0)


def in_vmem(n):
    return [pl.BlockSpec(memory_space=VM)] * n


def turn_weight(weight, ids, first):
    rows, cols = weight.shape
    toks = ids.shape[1]

    def body(f_ref, w_ref, i_ref, o_ref):
        o_ref[:cols, :] = w_ref[...].T.astype(bf16)
        number = lax.broadcasted_iota(jnp.int32, (DOCS, toks), 0)
        token = lax.broadcasted_iota(jnp.int32, (DOCS, toks), 1) + f_ref[0]
        found = jnp.where(i_ref[...] == number, token, NOWHERE).astype(f32)
        start = jnp.min(found, axis=1, keepdims=True)
        high = jnp.floor(start * (1.0 / 128.0))
        low = start - 128.0 * high
        digits = jnp.concatenate([high, low], axis=0)
        o_ref[cols:, :] = jnp.broadcast_to(digits, (NOTE, rows)).astype(bf16)

    return pl.pallas_call(
        body,
        in_specs=[SCALARS] + in_vmem(2),
        out_specs=pl.BlockSpec(memory_space=VM),
        out_shape=jax.ShapeDtypeStruct((cols + NOTE, rows), bf16),
        compiler_params=params(),
        cost_estimate=cost(0, rows * cols * 6),
    )(first, weight, ids)


def read_notes(*values):
    rows, width = values[0].shape[-2:]
    cols = rows - NOTE

    def body(*refs):
        least = None
        for ref in refs[:-1]:
            if len(ref.shape) == 2:
                notes = [ref[cols:, :]]
            else:
                notes = [ref[i, cols:, :] for i in range(ref.shape[0])]
            for note in notes:
                digits = note.astype(f32)
                start = 128.0 * digits[:DOCS] + digits[DOCS:]
                least = start if least is None else jnp.minimum(least, start)
        refs[-1][...] = least

    return pl.pallas_call(
        body,
        in_specs=in_vmem(len(values)),
        out_specs=pl.BlockSpec(memory_space=VM),
        out_shape=jax.ShapeDtypeStruct((DOCS, width), f32),
        compiler_params=params(),
        cost_estimate=cost(0, len(values) * 100000),
    )(*values)


def token_angles(base, notes, notes_sib, ids, ids_sib, freqs):
    toks = ids.shape[1]
    half = freqs.shape[0]

    def body(b_ref, n_ref, m_ref, i_ref, j_ref, f_ref, o_ref):
        starts = jnp.minimum(n_ref[...], m_ref[...])[:, :1]
        number = lax.broadcasted_iota(jnp.int32, (DOCS, toks), 0)
        token = lax.broadcasted_iota(jnp.int32, (1, toks), 1)
        for k, ref in enumerate((i_ref, j_ref)):
            began = jnp.sum(jnp.where(ref[...] == number, starts, 0.0), axis=0, keepdims=True)
            position = (token + b_ref[k]).astype(f32) - began
            o_ref[:, k * toks : (k + 1) * toks] = f_ref[...] * position

    return pl.pallas_call(
        body,
        in_specs=[SCALARS] + in_vmem(5),
        out_specs=pl.BlockSpec(memory_space=VM),
        out_shape=jax.ShapeDtypeStruct((half, 2 * toks), f32),
        compiler_params=params(),
        cost_estimate=cost(0, half * toks * 16),
    )(base, notes, notes_sib, ids, ids_sib, freqs)


def turn_target(target, target_sib, cosine, sine):
    toks, cols = target.shape
    half = HEAD // 2

    def body(t_ref, u_ref, c_ref, s_ref, o_ref):
        for k, ref in enumerate((t_ref, u_ref)):
            here = slice(k * toks, (k + 1) * toks)
            cosv, sinv = c_ref[:, here], s_ref[:, here]
            for head in range(cols // HEAD):
                at = head * HEAD
                turned = ref[:, at : at + HEAD].astype(f32).T
                u, w = turned[:half], turned[half:]
                o_ref[at : at + half, here] = u * cosv + w * sinv
                o_ref[at + half : at + HEAD, here] = w * cosv - u * sinv

    return pl.pallas_call(
        body,
        in_specs=in_vmem(4),
        out_specs=pl.BlockSpec(memory_space=VM),
        out_shape=jax.ShapeDtypeStruct((cols, 2 * toks), f32),
        compiler_params=params(),
        cost_estimate=cost(0, toks * cols * 12),
    )(target, target_sib, cosine, sine)


PART = 4


def pick_columns(features, blocks, blocks_sib, width):
    toks, depth = features.shape
    count = blocks.shape[0]
    rows = toks // 8

    def body(b_ref, d_ref, f_ref, o_ref, *s_refs):
        for k in range(count):
            at = pl.multiple_of(d_ref[k] * width, width)
            s_refs[k // PART][k % PART] = f_ref[:, pl.ds(at, width)]
        for k in range(count):
            at = pl.multiple_of(b_ref[k] * width, width)
            o_ref[k] = f_ref[:, pl.ds(at, width)]

    def stack(n):
        return jax.ShapeDtypeStruct((n, toks, width), features.dtype)

    def spec(n):
        return pl.BlockSpec((n, rows, width), lambda i, b, d: (0, i, 0))

    parts = count // PART
    out = pl.pallas_call(
        body,
        grid_spec=pltpu.PrefetchScalarGridSpec(
            num_scalar_prefetch=2,
            grid=(toks // rows,),
            in_specs=[pl.BlockSpec((rows, depth), lambda i, b, d: (i, 0))],
            out_specs=[spec(count)] + [spec(PART)] * parts,
        ),
        out_shape=[stack(count)] + [stack(PART)] * parts,
        compiler_params=params(),
        cost_estimate=cost(0, toks * count * width * 8),
    )(blocks, blocks_sib, features)
    return out[0], out[1:]


ANYWHERE = pl.BlockSpec(memory_space=pl.ANY)


def slab_buffers(n, toks, width):
    return [VM((2 * n, toks, width), bf16), pltpu.SemaphoreType.DMA((2 * n,))]


def parts_of(pieces, far):
    used = sorted({k // PART for k in pieces})
    return [far[p] for p in used], {k: used.index(k // PART) for k in pieces}


def start_copies(pieces, own_ref, far_refs, part, buf, sem):
    copies = []
    for k in pieces:
        for source in (own_ref.at[k], far_refs[part[k]].at[k % PART]):
            i = len(copies)
            copies.append(pltpu.make_async_copy(source, buf.at[i], sem.at[i]))
            copies[-1].start()
    return copies


def add_keys(pieces, own, far, weights, total):
    toks = own.shape[1]
    rows, width = weights[0].shape[-2:]
    cols = rows - NOTE
    m = len(weights)
    names = [k for held in pieces for k in held]
    n = len(names)
    held_far, part = parts_of(names, far)
    p = len(held_far)

    def body(own_ref, *refs):
        far_refs, refs = refs[:p], refs[p:]
        o_ref, buf, sem = refs[-3:]
        copies = start_copies(names, own_ref, far_refs, part, buf, sem)
        values = [None, None]
        if total is not None:
            values = [refs[m][:, :toks], refs[m][:, toks:]]
        i = 0
        for w_ref, held in zip(refs, pieces):
            for slab in range(len(held)):
                w = w_ref[:cols, :] if len(w_ref.shape) == 2 else w_ref[slab, :cols, :]
                for j in range(2):
                    copies[i].wait()
                    term = lax.dot_general(w, buf[i], NT, preferred_element_type=f32)
                    values[j] = term if values[j] is None else values[j] + term
                    i += 1
        o_ref[:, :toks] = values[0]
        o_ref[:, toks:] = values[1]

    extra = [] if total is None else [total]
    return pl.pallas_call(
        body,
        in_specs=[ANYWHERE] * (1 + p) + in_vmem(m + len(extra)),
        out_specs=pl.BlockSpec(memory_space=VM),
        out_shape=jax.ShapeDtypeStruct((cols, 2 * toks), f32),
        scratch_shapes=slab_buffers(n, toks, width),
        compiler_params=params(),
        cost_estimate=cost(4 * n * toks * cols * width, cols * toks * 8),
    )(own, *held_far, *weights, *extra)


def grads(pieces, own, far, back):
    toks, width = own.shape[1:]
    cols = back.shape[0]
    names = [k for held, _ in pieces for k in held]
    n = len(names)
    held_far, part = parts_of(names, far)
    p = len(held_far)

    def body(own_ref, *refs):
        far_refs, k_ref, refs = refs[:p], refs[p], refs[p + 1 :]
        buf, sem = refs[-2:]
        copies = start_copies(names, own_ref, far_refs, part, buf, sem)
        i = 0
        for o_ref, (held, kind) in zip(refs, pieces):
            for slab in range(len(held)):
                copies[i].wait()
                value = jnp.dot(k_ref[:, :toks], buf[i], preferred_element_type=f32)
                copies[i + 1].wait()
                value += jnp.dot(k_ref[:, toks:], buf[i + 1], preferred_element_type=f32)
                o_ref[slab] = value.astype(kind)
                i += 2

    return pl.pallas_call(
        body,
        in_specs=[ANYWHERE] * (1 + p) + in_vmem(1),
        out_specs=in_vmem(len(pieces)),
        out_shape=[jax.ShapeDtypeStruct((len(held), cols, width), kind) for held, kind in pieces],
        scratch_shapes=slab_buffers(n, toks, width),
        compiler_params=params(),
        cost_estimate=cost(4 * n * toks * cols * width, n * toks * width * 4),
    )(own, *held_far, back)


def first_grads(pieces, own, far, partial, partial_sib, turned, scales):
    toks, width = own.shape[1:]
    cols, both = partial.shape
    scale_keys, scale_back = scales
    n = len(pieces)
    held_far, part = parts_of(pieces, far)
    p = len(held_far)

    def body(own_ref, *refs):
        far_refs, (p_ref, q_ref, t_ref, k_ref, o_ref, buf, sem) = refs[:p], refs[p:]
        copies = start_copies(pieces, own_ref, far_refs, part, buf, sem)
        for here, there in ((slice(0, toks), slice(toks, both)), (slice(toks, both), slice(0, toks))):
            value = (p_ref[:, here] + q_ref[:, there]) * scale_keys - t_ref[:, here]
            k_ref[:, here] = (value * scale_back).astype(bf16)
        for i in range(n):
            copies[2 * i].wait()
            value = jnp.dot(k_ref[:, :toks], buf[2 * i], preferred_element_type=f32)
            copies[2 * i + 1].wait()
            value += jnp.dot(k_ref[:, toks:], buf[2 * i + 1], preferred_element_type=f32)
            o_ref[i] = value.astype(bf16)

    return pl.pallas_call(
        body,
        in_specs=[ANYWHERE] * (1 + p) + in_vmem(3),
        out_specs=in_vmem(2),
        out_shape=[
            jax.ShapeDtypeStruct((cols, both), bf16),
            jax.ShapeDtypeStruct((n, cols, width), bf16),
        ],
        scratch_shapes=slab_buffers(n, toks, width),
        compiler_params=params(),
        cost_estimate=cost(4 * n * toks * cols * width, cols * toks * 28),
    )(own, *held_far, partial, partial_sib, turned)


def combine(rows, kind, *values):
    shape = values[0].shape[-2:]

    def body(*refs):
        def term(i, slab):
            ref = refs[i]
            return (ref[...] if len(ref.shape) == 2 else ref[slab]).astype(f32)

        for slab, terms in enumerate(rows):
            value = term(*terms[0])
            for extra in terms[1:]:
                value = value + term(*extra)
            refs[-1][slab] = value.astype(kind)

    return pl.pallas_call(
        body,
        in_specs=in_vmem(len(values)),
        out_specs=pl.BlockSpec(memory_space=VM),
        out_shape=jax.ShapeDtypeStruct((len(rows),) + shape, kind),
        compiler_params=params(),
        cost_estimate=cost(0, len(rows) * shape[0] * shape[1] * 8),
    )(*values)


def fragment_delta(fragment, outer, weight):
    rows, width = outer.shape
    cols = width // FRAGS

    def body(g_ref, o_ref, w_ref, d_ref):
        for q in range(FRAGS):
            at = slice(q * cols, (q + 1) * cols)

            @pl.when(g_ref[0] == q)
            def _():
                d_ref[...] = o_ref[:, at] - w_ref[:, at]

    return pl.pallas_call(
        body,
        in_specs=[SCALARS] + in_vmem(2),
        out_specs=pl.BlockSpec(memory_space=VM),
        out_shape=jax.ShapeDtypeStruct((rows, cols), f32),
        compiler_params=params(),
        cost_estimate=cost(0, rows * cols * 12),
    )(fragment, outer, weight)


def outer_step(fragment, summed, outer, moment, replicas):
    rows, width = outer.shape
    cols = width // FRAGS

    def body(g_ref, d_ref, o_ref, m_ref, oo_ref, mo_ref):
        mean = d_ref[...] / replicas
        for q in range(FRAGS):
            at = slice(q * cols, (q + 1) * cols)
            here = g_ref[0] == q
            old, mom = o_ref[:, at], m_ref[:, at]
            mom_new = 0.9 * mom + mean
            mo_ref[:, at] = jnp.where(here, mom_new, mom)
            oo_ref[:, at] = jnp.where(here, old - 0.7 * (mean + 0.9 * mom_new), old)

    return pl.pallas_call(
        body,
        in_specs=[SCALARS] + in_vmem(3),
        out_specs=in_vmem(2),
        out_shape=[jax.ShapeDtypeStruct((rows, width), f32)] * 2,
        compiler_params=params(),
        cost_estimate=cost(0, rows * width * 16),
    )(fragment, summed, outer, moment)


def inner_step(fragment, parts, weight, first, second, outer_out):
    rows, width = weight.shape
    cols = width // FRAGS

    def body(g_ref, p0, p1, p2, w_ref, f_ref, s_ref, o_ref, inner, fo_ref, so_ref):
        for q in range(FRAGS):
            at = slice(q * cols, (q + 1) * cols)
            turned = p0[0, at, :] + p1[0, at, :].astype(f32) + p2[1, at, :].astype(f32)
            grad = turned.T
            fn = 0.9 * f_ref[:, at] + 0.1 * grad
            sn = 0.95 * s_ref[:, at] + 0.05 * grad * grad
            update = fn / first_fix / (jnp.sqrt(sn / second_fix) + 1e-08)
            w = w_ref[:, at]
            stepped = w - 0.02 * (update + 0.1 * w)
            fo_ref[:, at] = fn
            so_ref[:, at] = sn
            inner[:, at] = jnp.where(g_ref[0] == q, 0.5 * stepped + 0.5 * o_ref[:, at], stepped)

    return pl.pallas_call(
        body,
        in_specs=[SCALARS] + in_vmem(7),
        out_specs=in_vmem(3),
        out_shape=[jax.ShapeDtypeStruct((rows, width), f32)] * 3,
        compiler_params=params(),
        cost_estimate=cost(0, rows * width * 38),
    )(fragment, *parts, weight, first, second, outer_out)


def shards(
    acts,
    doc_ids,
    target,
    inner_weight,
    adam_first,
    adam_second,
    outer_weight,
    outer_moment,
    fragment,
):
    tok_count = acts.shape[1]
    group_tokens = tok_count * lax.axis_size("fsdp")
    features = acts[0]
    weight = inner_weight[0]
    width = weight.shape[0]
    me = lax.axis_index("fsdp")
    c, z, x = me % 2, (me // 2) % NZ, me // (2 * NZ)

    def column_blocks(core):
        s = way(core)

        def at(dx, dz, other):
            half = 1 - core if other else core
            return ((x + dx) % NX * NZ + (z + dz) % NZ) * 2 + half

        order = [at(0, 0, 0), at(s, 0, 0), at(s, 0, 1), at(2, 0, 0)]
        order += [at(0, s, 0), at(0, s, 1), at(s, s, 0), at(s, s, 1), at(2, s, 0)]
        order += [at(s, -s, 0), at(s, -s, 1), at(2, -s, 0)]
        order += [at(0, 2, 0), at(s, 2, 0), at(s, 2, 1), at(2, 2, 0)]
        return jnp.stack(order).astype(jnp.int32)

    blocks, blocks_sib = column_blocks(c), column_blocks(1 - c)

    base = jnp.stack([me, me ^ 1]).astype(jnp.int32) * tok_count

    replicas = lax.axis_size("replica")
    summed = fragment_delta(fragment, outer_weight, weight)

    def swapped(value, step):
        return value + lax.ppermute(value, "replica", [(r, r ^ step) for r in range(replicas)])

    def pair(first, i, second, j):
        return combine([[(0, i)], [(1, j)]], bf16, first, second)

    a0 = turn_weight(weight, doc_ids, base)
    b0 = move(a0, SIBLING)
    S0 = pair(a0, 0, b0, 0)
    X0 = move(S0, FROM_X)
    Z1 = move(S0, FROM_Z)
    own, share = pick_columns(features, after(blocks, S0), blocks_sib, width)
    F0 = move(after(X0[0], own), FROM_X)
    far0 = move(after(share[0], X0), SIBLING)
    Z1 = after(Z1, own)
    C1 = move(after(Z1, far0), SIBLING)
    X1 = move(Z1, FROM_X)
    a2 = move(Z1[0], FROM_Z)
    X2 = move(after(C1, F0), FROM_X)
    far1 = move(after(share[1], C1), SIBLING)
    far2 = move(after(share[2], C1), SIBLING)
    b2 = move(after(a2, X1), SIBLING)
    S3 = pair(a2, 0, b2, 0)
    X3 = move(S3, FROM_X)
    far3 = move(after(share[3], S3), SIBLING)
    ids_sib = move(after(doc_ids, S3), SIBLING)
    target_sib = move(after(target[0], S3), SIBLING)
    far = (far0, far1, far2, far3)
    keys = add_keys([(0,), (1, 2), (3,)], own, far, (a0, X0, F0), None)
    F12 = move(pair(X1, 0, after(X2, S3, keys), 1), FROM_X)
    keys = add_keys([(4, 5), (6, 7), (10, 9)], own, far, (Z1, X1, X2), keys)
    F2 = move(after(X3[0], keys), FROM_X)
    keys = add_keys([(12,), (13, 14), (8, 11)], own, far, (a2, X3, F12), keys)
    notes = read_notes(a0, X0, F0, Z1, X1, X2, a2, X3, F12, F2)
    notes_sib = move(notes, SIBLING)
    partial = add_keys([(15,)], own, far, (after(F2, notes, ids_sib, target_sib),), keys)
    partial_sib = move(after(partial, notes_sib), SIBLING)

    index = jnp.arange(HEAD // 2, dtype=f32)
    freqs = jnp.exp(index * f32(-2.0 * math.log(theta_base) / HEAD))[:, None]
    angles = token_angles(base, notes, notes_sib, doc_ids, ids_sib, freqs)
    turned = turn_target(target[0], target_sib, jnp.cos(angles), jnp.sin(angles))
    scales = (D ** (-0.5), group_tokens ** (-0.5))
    back, PF = first_grads((15, 8, 11, 3), own, far, partial, partial_sib, turned, scales)

    f = move(PF, TO_X)
    (P2,) = grads([((12, 13, 14), f32)], own, far, back)
    PM, PN = grads([((9, 10), f32), ((4, 5, 6, 7), f32)], own, far, after(back, P2))
    (P0,) = grads([((0, 1, 2), f32)], own, far, after(back, PN))
    summed = swapped(after(summed, back), 4)
    f = after(f, P0, summed)
    s2 = combine([[(0, 1), (1, 0)], [(0, 2)]], bf16, P2, f)
    g2 = move(s2, TO_X)
    s1 = combine(
        [[(1, 3)], [(0, 0), (2, 2)], [(1, 2), (2, 1)], [(0, 1)]], bf16, PM, PN, after(f, s2)
    )
    g1 = move(s1, TO_X)
    s0 = combine([[(0, 1), (1, 3)], [(0, 2)]], bf16, P0, after(f, s1))
    g0 = move(s0, TO_X)
    summed = swapped(after(summed, s0), 1)
    g2 = after(g2, s0, summed)
    s3 = combine([[(0, 0), (1, 0), (2, 1)]], bf16, P2, g2, move(g2, SIBLING))
    u2 = move(s3, TO_Z)
    summed = swapped(after(summed, s3), 2)
    outer_out, moment_out = outer_step(fragment, summed, outer_weight, outer_moment, replicas)
    g1 = after(g1, u2, outer_out)
    c1 = move(g1, SIBLING)
    s4 = combine(
        [[(0, 0), (1, 2), (2, 3), (3, 0)], [(0, 1), (1, 0), (2, 1)]], bf16, PN, g1, c1, u2
    )
    h = move(s4, TO_Z)
    g0 = after(g0, s4)
    mine = combine([[(0, 0), (1, 0), (2, 1)]], f32, P0, g0, move(g0, SIBLING))
    inner_out, first_out, second_out = inner_step(
        fragment, (mine, h, move(h, SIBLING)), weight, adam_first[0], adam_second[0], outer_out
    )
    return (inner_out[None], first_out[None], second_out[None], outer_out, moment_out)


def solution(mesh):
    in_specs = (
        P("replica", "fsdp", None),
        P("replica", "fsdp"),
        P("replica", "fsdp", None),
        P("replica", "fsdp", None),
        P("replica", "fsdp", None),
        P("replica", "fsdp", None),
        P("fsdp", None),
        P("fsdp", None),
        P(),
    )
    out_specs = (
        P("replica", "fsdp", None),
        P("replica", "fsdp", None),
        P("replica", "fsdp", None),
        P("fsdp", None),
        P("fsdp", None),
    )
    return jax.shard_map(shards, mesh=mesh, in_specs=in_specs, out_specs=out_specs, check_vma=False)
```

```python
import math

import jax
import jax.numpy as jnp
from jax import lax
from jax.experimental import pallas as pl
from jax.experimental.pallas import tpu as pltpu
from jax.sharding import PartitionSpec as P

D = 8192
HEAD = 128
FRAGS = 4
DOCS = 8

theta_base = 500000.0
first_fix = 0.9999734386011124
second_fix = 0.9940794707796672

f32 = jnp.float32
bf16 = jnp.bfloat16
VM = pltpu.VMEM
LIMIT = 16 * 1024 * 1024
NOTE = 16
NOWHERE = 128 * 255
NT = (((1,), (1,)), ((), ()))
SCALARS = pl.BlockSpec(memory_space=pltpu.SMEM)

NX, NZ = 4, 4
TORUS = [(x, z, c) for x in range(NX) for z in range(NZ) for c in range(2)]


def place(x, z, c):
    return ((x % NX) * NZ + z % NZ) * 2 + c


def pairs(target):
    return [(place(*at), place(*target(*at))) for at in TORUS]


def way(c):
    return 1 - 2 * c


FROM_X = pairs(lambda x, z, c: (x - way(c), z, c))
FROM_Z = pairs(lambda x, z, c: (x, z - way(c), c))
TO_X = pairs(lambda x, z, c: (x + way(c), z, c))
TO_Z = pairs(lambda x, z, c: (x, z + way(c), c))
SIBLING = pairs(lambda x, z, c: (x, z, 1 - c))


def move(value, table):
    return lax.ppermute(value, "fsdp", table)


def after(value, *others):
    return lax.optimization_barrier((value,) + others)[0]


def params(limit=LIMIT):
    return pltpu.CompilerParams(vmem_limit_bytes=limit)


def cost(flops, moved):
    return pl.CostEstimate(flops=flops, bytes_accessed=moved, transcendentals=0)


def in_vmem(n):
    return [pl.BlockSpec(memory_space=VM)] * n


def turn_weight(weight, ids, first):
    rows, cols = weight.shape
    toks = ids.shape[1]

    def body(f_ref, w_ref, i_ref, o_ref):
        o_ref[:cols, :] = w_ref[...].T.astype(bf16)
        number = lax.broadcasted_iota(jnp.int32, (DOCS, toks), 0)
        token = lax.broadcasted_iota(jnp.int32, (DOCS, toks), 1) + f_ref[0]
        found = jnp.where(i_ref[...] == number, token, NOWHERE).astype(f32)
        start = jnp.min(found, axis=1, keepdims=True)
        high = jnp.floor(start * (1.0 / 128.0))
        low = start - 128.0 * high
        digits = jnp.concatenate([high, low], axis=0)
        o_ref[cols:, :] = jnp.broadcast_to(digits, (NOTE, rows)).astype(bf16)

    return pl.pallas_call(
        body,
        in_specs=[SCALARS] + in_vmem(2),
        out_specs=pl.BlockSpec(memory_space=VM),
        out_shape=jax.ShapeDtypeStruct((cols + NOTE, rows), bf16),
        compiler_params=params(),
        cost_estimate=cost(0, rows * cols * 6),
    )(first, weight, ids)


def read_notes(*values):
    rows, width = values[0].shape[-2:]
    cols = rows - NOTE

    def body(*refs):
        least = None
        for ref in refs[:-1]:
            if len(ref.shape) == 2:
                notes = [ref[cols:, :]]
            else:
                notes = [ref[i, cols:, :] for i in range(ref.shape[0])]
            for note in notes:
                digits = note.astype(f32)
                start = 128.0 * digits[:DOCS] + digits[DOCS:]
                least = start if least is None else jnp.minimum(least, start)
        refs[-1][...] = least

    return pl.pallas_call(
        body,
        in_specs=in_vmem(len(values)),
        out_specs=pl.BlockSpec(memory_space=VM),
        out_shape=jax.ShapeDtypeStruct((DOCS, width), f32),
        compiler_params=params(),
        cost_estimate=cost(0, len(values) * 100000),
    )(*values)


def token_angles(base, notes, notes_sib, ids, ids_sib, freqs):
    toks = ids.shape[1]
    half = freqs.shape[0]

    def body(b_ref, n_ref, m_ref, i_ref, j_ref, f_ref, o_ref):
        starts = jnp.minimum(n_ref[...], m_ref[...])[:, :1]
        number = lax.broadcasted_iota(jnp.int32, (DOCS, toks), 0)
        token = lax.broadcasted_iota(jnp.int32, (1, toks), 1)
        for k, ref in enumerate((i_ref, j_ref)):
            began = jnp.sum(jnp.where(ref[...] == number, starts, 0.0), axis=0, keepdims=True)
            position = (token + b_ref[k]).astype(f32) - began
            o_ref[:, k * toks : (k + 1) * toks] = f_ref[...] * position

    return pl.pallas_call(
        body,
        in_specs=[SCALARS] + in_vmem(5),
        out_specs=pl.BlockSpec(memory_space=VM),
        out_shape=jax.ShapeDtypeStruct((half, 2 * toks), f32),
        compiler_params=params(),
        cost_estimate=cost(0, half * toks * 16),
    )(base, notes, notes_sib, ids, ids_sib, freqs)


def turn_target(target, target_sib, cosine, sine):
    toks, cols = target.shape
    half = HEAD // 2

    def body(t_ref, u_ref, c_ref, s_ref, o_ref):
        for k, ref in enumerate((t_ref, u_ref)):
            here = slice(k * toks, (k + 1) * toks)
            cosv, sinv = c_ref[:, here], s_ref[:, here]
            for head in range(cols // HEAD):
                at = head * HEAD
                turned = ref[:, at : at + HEAD].astype(f32).T
                u, w = turned[:half], turned[half:]
                o_ref[at : at + half, here] = u * cosv + w * sinv
                o_ref[at + half : at + HEAD, here] = w * cosv - u * sinv

    return pl.pallas_call(
        body,
        in_specs=in_vmem(4),
        out_specs=pl.BlockSpec(memory_space=VM),
        out_shape=jax.ShapeDtypeStruct((cols, 2 * toks), f32),
        compiler_params=params(),
        cost_estimate=cost(0, toks * cols * 12),
    )(target, target_sib, cosine, sine)


PART = 4


def pick_columns(features, blocks, blocks_sib, width):
    toks, depth = features.shape
    count = blocks.shape[0]
    rows = toks // 8

    def body(b_ref, d_ref, f_ref, o_ref, *s_refs):
        for k in range(count):
            at = pl.multiple_of(d_ref[k] * width, width)
            s_refs[k // PART][k % PART] = f_ref[:, pl.ds(at, width)]
        for k in range(count):
            at = pl.multiple_of(b_ref[k] * width, width)
            o_ref[k] = f_ref[:, pl.ds(at, width)]

    def stack(n):
        return jax.ShapeDtypeStruct((n, toks, width), features.dtype)

    def spec(n):
        return pl.BlockSpec((n, rows, width), lambda i, b, d: (0, i, 0))

    parts = count // PART
    out = pl.pallas_call(
        body,
        grid_spec=pltpu.PrefetchScalarGridSpec(
            num_scalar_prefetch=2,
            grid=(toks // rows,),
            in_specs=[pl.BlockSpec((rows, depth), lambda i, b, d: (i, 0))],
            out_specs=[spec(count)] + [spec(PART)] * parts,
        ),
        out_shape=[stack(count)] + [stack(PART)] * parts,
        compiler_params=params(),
        cost_estimate=cost(0, toks * count * width * 8),
    )(blocks, blocks_sib, features)
    return out[0], out[1:]


def parts_of(pieces, far):
    used = sorted({k // PART for k in pieces})
    return [far[p] for p in used], {k: used.index(k // PART) for k in pieces}


def add_keys(pieces, own, far, weights, total):
    toks = own.shape[1]
    rows, width = weights[0].shape[-2:]
    cols = rows - NOTE
    m = len(weights)
    names = [k for held in pieces for k in held]
    n = len(names)
    held_far, part = parts_of(names, far)
    p = len(held_far)

    def body(own_ref, *refs):
        far_refs, refs = refs[:p], refs[p:]
        o_ref = refs[-1]
        values = [None, None]
        if total is not None:
            values = [refs[m][:, :toks], refs[m][:, toks:]]
        for w_ref, held in zip(refs, pieces):
            for slab, k in enumerate(held):
                w = w_ref[:cols, :] if len(w_ref.shape) == 2 else w_ref[slab, :cols, :]
                for j, block in enumerate((own_ref[k], far_refs[part[k]][k % PART])):
                    term = lax.dot_general(w, block, NT, preferred_element_type=f32)
                    values[j] = term if values[j] is None else values[j] + term
        o_ref[:, :toks] = values[0]
        o_ref[:, toks:] = values[1]

    extra = [] if total is None else [total]
    return pl.pallas_call(
        body,
        in_specs=in_vmem(1 + p + m + len(extra)),
        out_specs=pl.BlockSpec(memory_space=VM),
        out_shape=jax.ShapeDtypeStruct((cols, 2 * toks), f32),
        compiler_params=params(),
        cost_estimate=cost(4 * n * toks * cols * width, cols * toks * 8),
    )(own, *held_far, *weights, *extra)


def grads(pieces, own, far, back):
    toks, width = own.shape[1:]
    cols = back.shape[0]
    names = [k for held, _ in pieces for k in held]
    n = len(names)
    held_far, part = parts_of(names, far)
    p = len(held_far)

    def body(own_ref, *refs):
        far_refs, k_ref, refs = refs[:p], refs[p], refs[p + 1 :]
        for o_ref, (held, kind) in zip(refs, pieces):
            for slab, k in enumerate(held):
                value = jnp.dot(k_ref[:, :toks], own_ref[k], preferred_element_type=f32)
                block = far_refs[part[k]][k % PART]
                value += jnp.dot(k_ref[:, toks:], block, preferred_element_type=f32)
                o_ref[slab] = value.astype(kind)

    return pl.pallas_call(
        body,
        in_specs=in_vmem(2 + p),
        out_specs=in_vmem(len(pieces)),
        out_shape=[jax.ShapeDtypeStruct((len(held), cols, width), kind) for held, kind in pieces],
        compiler_params=params(),
        cost_estimate=cost(4 * n * toks * cols * width, n * toks * width * 4),
    )(own, *held_far, back)


def first_grads(groups, own, far, partial, partial_sib, turned, scales):
    toks, width = own.shape[1:]
    cols, both = partial.shape
    scale_keys, scale_back = scales
    pieces = [k for group in groups for k in group]
    n = len(pieces)
    held_far, part = parts_of(pieces, far)
    p = len(held_far)

    def body(own_ref, *refs):
        far_refs, (p_ref, q_ref, t_ref, k_ref), refs = refs[:p], refs[p : p + 4], refs[p + 4 :]
        for here, there in ((slice(0, toks), slice(toks, both)), (slice(toks, both), slice(0, toks))):
            value = (p_ref[:, here] + q_ref[:, there]) * scale_keys - t_ref[:, here]
            k_ref[:, here] = (value * scale_back).astype(bf16)
        for o_ref, group in zip(refs, groups):
            for slab, k in enumerate(group):
                value = jnp.dot(k_ref[:, :toks], own_ref[k], preferred_element_type=f32)
                block = far_refs[part[k]][k % PART]
                value += jnp.dot(k_ref[:, toks:], block, preferred_element_type=f32)
                o_ref[slab] = value.astype(bf16)

    return pl.pallas_call(
        body,
        in_specs=in_vmem(4 + p),
        out_specs=in_vmem(1 + len(groups)),
        out_shape=[jax.ShapeDtypeStruct((cols, both), bf16)]
        + [jax.ShapeDtypeStruct((len(group), cols, width), bf16) for group in groups],
        compiler_params=params(),
        cost_estimate=cost(4 * n * toks * cols * width, cols * toks * 28),
    )(own, *held_far, partial, partial_sib, turned)


def combine(rows, kind, *values):
    shape = values[0].shape[-2:]

    def body(*refs):
        def term(i, slab):
            ref = refs[i]
            return (ref[...] if len(ref.shape) == 2 else ref[slab]).astype(f32)

        for slab, terms in enumerate(rows):
            value = term(*terms[0])
            for extra in terms[1:]:
                value = value + term(*extra)
            refs[-1][slab] = value.astype(kind)

    return pl.pallas_call(
        body,
        in_specs=in_vmem(len(values)),
        out_specs=pl.BlockSpec(memory_space=VM),
        out_shape=jax.ShapeDtypeStruct((len(rows),) + shape, kind),
        compiler_params=params(),
        cost_estimate=cost(0, len(rows) * shape[0] * shape[1] * 8),
    )(*values)


def fragment_delta(fragment, outer, weight):
    rows, width = outer.shape
    cols = width // FRAGS

    def body(g_ref, o_ref, w_ref, d_ref):
        for q in range(FRAGS):
            at = slice(q * cols, (q + 1) * cols)

            @pl.when(g_ref[0] == q)
            def _():
                d_ref[...] = o_ref[:, at] - w_ref[:, at]

    return pl.pallas_call(
        body,
        in_specs=[SCALARS] + in_vmem(2),
        out_specs=pl.BlockSpec(memory_space=VM),
        out_shape=jax.ShapeDtypeStruct((rows, cols), f32),
        compiler_params=params(),
        cost_estimate=cost(0, rows * cols * 12),
    )(fragment, outer, weight)


def outer_step(fragment, summed, outer, moment, replicas):
    rows, width = outer.shape
    cols = width // FRAGS

    def body(g_ref, d_ref, o_ref, m_ref, oo_ref, mo_ref):
        mean = d_ref[...] / replicas
        for q in range(FRAGS):
            at = slice(q * cols, (q + 1) * cols)
            here = g_ref[0] == q
            old, mom = o_ref[:, at], m_ref[:, at]
            mom_new = 0.9 * mom + mean
            mo_ref[:, at] = jnp.where(here, mom_new, mom)
            oo_ref[:, at] = jnp.where(here, old - 0.7 * (mean + 0.9 * mom_new), old)

    return pl.pallas_call(
        body,
        in_specs=[SCALARS] + in_vmem(3),
        out_specs=in_vmem(2),
        out_shape=[jax.ShapeDtypeStruct((rows, width), f32)] * 2,
        compiler_params=params(),
        cost_estimate=cost(0, rows * width * 16),
    )(fragment, summed, outer, moment)


def inner_step(fragment, parts, weight, first, second, outer_out):
    rows, width = weight.shape
    cols = width // FRAGS

    def body(g_ref, p0, p1, p2, w_ref, f_ref, s_ref, o_ref, inner, fo_ref, so_ref):
        for q in range(FRAGS):
            at = slice(q * cols, (q + 1) * cols)
            turned = p0[0, at, :] + p1[0, at, :].astype(f32) + p2[1, at, :].astype(f32)
            grad = turned.T
            fn = 0.9 * f_ref[:, at] + 0.1 * grad
            sn = 0.95 * s_ref[:, at] + 0.05 * grad * grad
            update = fn / first_fix / (jnp.sqrt(sn / second_fix) + 1e-08)
            w = w_ref[:, at]
            stepped = w - 0.02 * (update + 0.1 * w)
            fo_ref[:, at] = fn
            so_ref[:, at] = sn
            inner[:, at] = jnp.where(g_ref[0] == q, 0.5 * stepped + 0.5 * o_ref[:, at], stepped)

    return pl.pallas_call(
        body,
        in_specs=[SCALARS] + in_vmem(7),
        out_specs=in_vmem(3),
        out_shape=[jax.ShapeDtypeStruct((rows, width), f32)] * 3,
        compiler_params=params(),
        cost_estimate=cost(0, rows * width * 38),
    )(fragment, *parts, weight, first, second, outer_out)


def shards(
    acts,
    doc_ids,
    target,
    inner_weight,
    adam_first,
    adam_second,
    outer_weight,
    outer_moment,
    fragment,
):
    tok_count = acts.shape[1]
    group_tokens = tok_count * lax.axis_size("fsdp")
    features = acts[0]
    weight = inner_weight[0]
    width = weight.shape[0]
    me = lax.axis_index("fsdp")
    c, z, x = me % 2, (me // 2) % NZ, me // (2 * NZ)

    def column_blocks(core):
        s = way(core)

        def at(dx, dz, other):
            half = 1 - core if other else core
            return ((x + dx) % NX * NZ + (z + dz) % NZ) * 2 + half

        order = [at(0, 0, 0), at(s, 0, 0), at(s, 0, 1), at(2, 0, 0)]
        order += [at(0, s, 0), at(0, s, 1), at(s, s, 0), at(s, s, 1), at(2, s, 0)]
        order += [at(s, -s, 0), at(s, -s, 1), at(2, -s, 0)]
        order += [at(0, 2, 0), at(s, 2, 0), at(s, 2, 1), at(2, 2, 0)]
        return jnp.stack(order).astype(jnp.int32)

    blocks, blocks_sib = column_blocks(c), column_blocks(1 - c)

    base = jnp.stack([me, me ^ 1]).astype(jnp.int32) * tok_count

    replicas = lax.axis_size("replica")
    summed = fragment_delta(fragment, outer_weight, weight)

    def swapped(value, step):
        return value + lax.ppermute(value, "replica", [(r, r ^ step) for r in range(replicas)])

    def pair(first, i, second, j):
        return combine([[(0, i)], [(1, j)]], bf16, first, second)

    def together(*values):
        return lax.optimization_barrier(values)

    a0 = turn_weight(weight, doc_ids, base)
    b0 = move(a0, SIBLING)
    S0 = pair(a0, 0, b0, 0)
    X0 = move(S0, FROM_X)
    Z1 = move(S0, FROM_Z)
    own, share = pick_columns(features, after(blocks, S0), blocks_sib, width)
    F0 = move(after(X0[0], own), FROM_X)
    X0, Z1, F0, own, summed, *share = together(X0, Z1, F0, own, summed, *share)

    C1 = move(Z1, SIBLING)
    X1 = move(Z1, FROM_X)
    a2 = move(Z1[0], FROM_Z)
    X2 = move(C1, FROM_X)
    far0 = move(after(share[0], C1), SIBLING)
    far1 = move(after(share[1], C1), SIBLING)
    b2 = move(after(a2, X1), SIBLING)
    X1, X2, a2, b2, far0, far1, *share = together(X1, X2, a2, b2, far0, far1, *share)

    F12 = move(pair(X1, 0, X2, 1), FROM_X)
    S3 = pair(a2, 0, b2, 0)
    X3 = move(S3, FROM_X)
    far2 = move(share[2], SIBLING)
    far3 = move(share[3], SIBLING)
    ids_sib = move(after(doc_ids, b2), SIBLING)
    target_sib = move(after(target[0], b2), SIBLING)
    far = (far0, far1, far2, far3)
    keys = add_keys([(0,), (1, 2), (3,)], own, far, (a0, X0, F0), None)
    keys = add_keys([(4, 5), (6, 7), (10, 9)], own, far, (Z1, X1, X2), keys)
    summed = swapped(after(summed, b2), 4)
    X3, F12, keys, ids_sib, target_sib, summed = together(
        X3, F12, keys, ids_sib, target_sib, summed
    )

    F2 = move(X3[0], FROM_X)
    keys = add_keys([(12,), (13, 14), (8, 11)], own, far, (a2, X3, F12), keys)
    F2, keys = together(F2, keys)
    notes = read_notes(a0, X0, F0, Z1, X1, X2, a2, X3, F12, F2)
    notes_sib = move(notes, SIBLING)
    partial = add_keys([(15,)], own, far, (after(F2, notes),), keys)
    partial_sib = move(after(partial, notes_sib), SIBLING)

    index = jnp.arange(HEAD // 2, dtype=f32)
    freqs = jnp.exp(index * f32(-2.0 * math.log(theta_base) / HEAD))[:, None]
    angles = token_angles(base, notes, notes_sib, doc_ids, ids_sib, freqs)
    turned = turn_target(target[0], target_sib, jnp.cos(angles), jnp.sin(angles))
    scales = (D ** (-0.5), group_tokens ** (-0.5))
    back, PF2 = first_grads(((15,),), own, far, partial, partial_sib, turned, scales)

    f2 = move(PF2, TO_X)
    PF1, P2 = grads([((8, 11), bf16), ((12, 13, 14), f32)], own, far, back)
    f1 = move(PF1, TO_X)
    summed = swapped(after(summed, back), 1)
    s2 = combine([[(0, 1), (1, 0)], [(0, 2)]], bf16, P2, f2)
    g2 = move(s2, TO_X)
    PM, PN = grads([((9, 10), f32), ((4, 5, 6, 7), f32)], own, far, after(back, s2))
    f1 = after(f1, PN, summed)
    s1 = combine([[(1, 3)], [(0, 0), (2, 1)], [(1, 2), (2, 0)], [(0, 1)]], bf16, PM, PN, f1)
    g1 = move(s1, TO_X)
    P0, PF0 = grads([((0, 1, 2), f32), ((3,), bf16)], own, far, after(back, s1))
    f0 = move(PF0, TO_X)
    g2, s1 = together(g2, s1)
    s3 = combine([[(0, 0), (1, 0), (2, 1)]], bf16, P2, g2, move(g2, SIBLING))
    u2 = move(s3, TO_Z)
    summed = swapped(after(summed, s3), 2)
    g1, u2, f0, summed = together(g1, u2, f0, summed)
    c1 = move(g1, SIBLING)
    s4 = combine(
        [[(0, 0), (1, 2), (2, 3), (3, 0)], [(0, 1), (1, 0), (2, 1)]], bf16, PN, g1, c1, u2
    )
    h = move(s4, TO_Z)
    s0 = combine([[(0, 1), (1, 0)], [(0, 2)]], bf16, P0, after(f0, s4))
    g0 = move(s0, TO_X)
    outer_out, moment_out = outer_step(
        fragment, after(summed, s0), outer_weight, outer_moment, replicas
    )
    g0, h = together(g0, h)
    mine = combine([[(0, 0), (1, 0), (2, 1)]], f32, P0, g0, move(g0, SIBLING))
    inner_out, first_out, second_out = inner_step(
        fragment, (mine, h, move(h, SIBLING)), weight, adam_first[0], adam_second[0], outer_out
    )
    return (inner_out[None], first_out[None], second_out[None], outer_out, moment_out)


def solution(mesh):
    in_specs = (
        P("replica", "fsdp", None),
        P("replica", "fsdp"),
        P("replica", "fsdp", None),
        P("replica", "fsdp", None),
        P("replica", "fsdp", None),
        P("replica", "fsdp", None),
        P("fsdp", None),
        P("fsdp", None),
        P(),
    )
    out_specs = (
        P("replica", "fsdp", None),
        P("replica", "fsdp", None),
        P("replica", "fsdp", None),
        P("fsdp", None),
        P("fsdp", None),
    )
    return jax.shard_map(shards, mesh=mesh, in_specs=in_specs, out_specs=out_specs, check_vma=False)
```

```python
import math

import jax
import jax.numpy as jnp
from jax import lax
from jax.experimental import pallas as pl
from jax.experimental.pallas import tpu as pltpu
from jax.sharding import PartitionSpec as P

D = 8192
HEAD = 128
FRAGS = 4
DOCS = 8

theta_base = 500000.0
first_fix = 0.9999734386011124
second_fix = 0.9940794707796672

f32 = jnp.float32
bf16 = jnp.bfloat16
VM = pltpu.VMEM
LIMIT = 16 * 1024 * 1024
NOTE = 16
NOWHERE = 128 * 255
NT = (((1,), (1,)), ((), ()))
SCALARS = pl.BlockSpec(memory_space=pltpu.SMEM)

NX, NZ = 4, 4
TORUS = [(x, z, c) for x in range(NX) for z in range(NZ) for c in range(2)]


def place(x, z, c):
    return ((x % NX) * NZ + z % NZ) * 2 + c


def pairs(target):
    return [(place(*at), place(*target(*at))) for at in TORUS]


def way(c):
    return 1 - 2 * c


FROM_X = pairs(lambda x, z, c: (x - way(c), z, c))
FROM_Z = pairs(lambda x, z, c: (x, z - way(c), c))
TO_X = pairs(lambda x, z, c: (x + way(c), z, c))
TO_Z = pairs(lambda x, z, c: (x, z + way(c), c))
SIBLING = pairs(lambda x, z, c: (x, z, 1 - c))


def move(value, table):
    return lax.ppermute(value, "fsdp", table)


def after(value, *others):
    return lax.optimization_barrier((value,) + others)[0]


def params(limit=LIMIT):
    return pltpu.CompilerParams(vmem_limit_bytes=limit)


def cost(flops, moved):
    return pl.CostEstimate(flops=flops, bytes_accessed=moved, transcendentals=0)


def in_vmem(n):
    return [pl.BlockSpec(memory_space=VM)] * n


def turn_weight(weight, ids, first):
    rows, cols = weight.shape
    toks = ids.shape[1]

    def body(f_ref, w_ref, i_ref, o_ref):
        o_ref[:cols, :] = w_ref[...].T.astype(bf16)
        number = lax.broadcasted_iota(jnp.int32, (DOCS, toks), 0)
        token = lax.broadcasted_iota(jnp.int32, (DOCS, toks), 1) + f_ref[0]
        found = jnp.where(i_ref[...] == number, token, NOWHERE).astype(f32)
        start = jnp.min(found, axis=1, keepdims=True)
        high = jnp.floor(start * (1.0 / 128.0))
        low = start - 128.0 * high
        digits = jnp.concatenate([high, low], axis=0)
        o_ref[cols:, :] = jnp.broadcast_to(digits, (NOTE, rows)).astype(bf16)

    return pl.pallas_call(
        body,
        in_specs=[SCALARS] + in_vmem(2),
        out_specs=pl.BlockSpec(memory_space=VM),
        out_shape=jax.ShapeDtypeStruct((cols + NOTE, rows), bf16),
        compiler_params=params(),
        cost_estimate=cost(0, rows * cols * 6),
    )(first, weight, ids)


def read_notes(*values):
    rows, width = values[0].shape[-2:]
    cols = rows - NOTE

    def body(*refs):
        least = None
        for ref in refs[:-1]:
            if len(ref.shape) == 2:
                notes = [ref[cols:, :]]
            else:
                notes = [ref[i, cols:, :] for i in range(ref.shape[0])]
            for note in notes:
                digits = note.astype(f32)
                start = 128.0 * digits[:DOCS] + digits[DOCS:]
                least = start if least is None else jnp.minimum(least, start)
        refs[-1][...] = least

    return pl.pallas_call(
        body,
        in_specs=in_vmem(len(values)),
        out_specs=pl.BlockSpec(memory_space=VM),
        out_shape=jax.ShapeDtypeStruct((DOCS, width), f32),
        compiler_params=params(),
        cost_estimate=cost(0, len(values) * 100000),
    )(*values)


def token_angles(base, notes, notes_sib, ids, ids_sib, freqs):
    toks = ids.shape[1]
    half = freqs.shape[0]

    def body(b_ref, n_ref, m_ref, i_ref, j_ref, f_ref, o_ref):
        starts = jnp.minimum(n_ref[...], m_ref[...])[:, :1]
        number = lax.broadcasted_iota(jnp.int32, (DOCS, toks), 0)
        token = lax.broadcasted_iota(jnp.int32, (1, toks), 1)
        for k, ref in enumerate((i_ref, j_ref)):
            began = jnp.sum(jnp.where(ref[...] == number, starts, 0.0), axis=0, keepdims=True)
            position = (token + b_ref[k]).astype(f32) - began
            o_ref[:, k * toks : (k + 1) * toks] = f_ref[...] * position

    return pl.pallas_call(
        body,
        in_specs=[SCALARS] + in_vmem(5),
        out_specs=pl.BlockSpec(memory_space=VM),
        out_shape=jax.ShapeDtypeStruct((half, 2 * toks), f32),
        compiler_params=params(),
        cost_estimate=cost(0, half * toks * 16),
    )(base, notes, notes_sib, ids, ids_sib, freqs)


def turn_target(target, target_sib, cosine, sine):
    toks, cols = target.shape
    half = HEAD // 2

    def body(t_ref, u_ref, c_ref, s_ref, o_ref):
        for k, ref in enumerate((t_ref, u_ref)):
            here = slice(k * toks, (k + 1) * toks)
            cosv, sinv = c_ref[:, here], s_ref[:, here]
            for head in range(cols // HEAD):
                at = head * HEAD
                turned = ref[:, at : at + HEAD].astype(f32).T
                u, w = turned[:half], turned[half:]
                o_ref[at : at + half, here] = u * cosv + w * sinv
                o_ref[at + half : at + HEAD, here] = w * cosv - u * sinv

    return pl.pallas_call(
        body,
        in_specs=in_vmem(4),
        out_specs=pl.BlockSpec(memory_space=VM),
        out_shape=jax.ShapeDtypeStruct((cols, 2 * toks), f32),
        compiler_params=params(),
        cost_estimate=cost(0, toks * cols * 12),
    )(target, target_sib, cosine, sine)


PART = 4


def pick_columns(features, blocks, blocks_sib, width):
    toks, depth = features.shape
    count = blocks.shape[0]
    rows = toks // 8

    def body(b_ref, d_ref, f_ref, o_ref, *s_refs):
        for k in range(count):
            at = pl.multiple_of(d_ref[k] * width, width)
            s_refs[k // PART][k % PART] = f_ref[:, pl.ds(at, width)]
        for k in range(count):
            at = pl.multiple_of(b_ref[k] * width, width)
            o_ref[k] = f_ref[:, pl.ds(at, width)]

    def stack(n):
        return jax.ShapeDtypeStruct((n, toks, width), features.dtype)

    def spec(n):
        return pl.BlockSpec((n, rows, width), lambda i, b, d: (0, i, 0))

    parts = count // PART
    out = pl.pallas_call(
        body,
        grid_spec=pltpu.PrefetchScalarGridSpec(
            num_scalar_prefetch=2,
            grid=(toks // rows,),
            in_specs=[pl.BlockSpec((rows, depth), lambda i, b, d: (i, 0))],
            out_specs=[spec(count)] + [spec(PART)] * parts,
        ),
        out_shape=[stack(count)] + [stack(PART)] * parts,
        compiler_params=params(),
        cost_estimate=cost(0, toks * count * width * 8),
    )(blocks, blocks_sib, features)
    return out[0], out[1:]


def parts_of(pieces, far):
    used = sorted({k // PART for k in pieces})
    return [far[p] for p in used], {k: used.index(k // PART) for k in pieces}


def add_keys(pieces, own, far, weights, total, send=False):
    toks = own.shape[1]
    rows, width = weights[0].shape[-2:]
    cols = rows - NOTE
    m = len(weights)
    names = [k for held in pieces for k in held]
    n = len(names)
    held_far, part = parts_of(names, far)
    p = len(held_far)
    extra = [] if total is None else [total]

    def body(own_ref, *refs):
        far_refs, refs = refs[:p], refs[p:]
        o_ref = refs[m + len(extra)]
        values = [None, None]
        if total is not None:
            values = [refs[m][:, :toks], refs[m][:, toks:]]
        for w_ref, held in zip(refs, pieces):
            for slab, k in enumerate(held):
                w = w_ref[:cols, :] if len(w_ref.shape) == 2 else w_ref[slab, :cols, :]
                for j, block in enumerate((own_ref[k], far_refs[part[k]][k % PART])):
                    term = lax.dot_general(w, block, NT, preferred_element_type=f32)
                    values[j] = term if values[j] is None else values[j] + term
        o_ref[:, :toks] = values[0]
        o_ref[:, toks:] = values[1]
        if send:
            refs[-1][:, :toks] = values[0].astype(bf16)
            refs[-1][:, toks:] = values[1].astype(bf16)

    kinds = [f32, bf16] if send else [f32]
    out = pl.pallas_call(
        body,
        in_specs=in_vmem(1 + p + m + len(extra)),
        out_specs=in_vmem(len(kinds)),
        out_shape=[jax.ShapeDtypeStruct((cols, 2 * toks), kind) for kind in kinds],
        compiler_params=params(),
        cost_estimate=cost(4 * n * toks * cols * width, cols * toks * 8),
    )(own, *held_far, *weights, *extra)
    return out if send else out[0]


def grads(pieces, own, far, back):
    toks, width = own.shape[1:]
    cols = back.shape[0]
    names = [k for held, _ in pieces for k in held]
    n = len(names)
    held_far, part = parts_of(names, far)
    p = len(held_far)

    def body(own_ref, *refs):
        far_refs, k_ref, refs = refs[:p], refs[p], refs[p + 1 :]
        for o_ref, (held, kind) in zip(refs, pieces):
            for slab, k in enumerate(held):
                value = jnp.dot(k_ref[:, :toks], own_ref[k], preferred_element_type=f32)
                block = far_refs[part[k]][k % PART]
                value += jnp.dot(k_ref[:, toks:], block, preferred_element_type=f32)
                o_ref[slab] = value.astype(kind)

    return pl.pallas_call(
        body,
        in_specs=in_vmem(2 + p),
        out_specs=in_vmem(len(pieces)),
        out_shape=[jax.ShapeDtypeStruct((len(held), cols, width), kind) for held, kind in pieces],
        compiler_params=params(),
        cost_estimate=cost(4 * n * toks * cols * width, n * toks * width * 4),
    )(own, *held_far, back)


def first_grads(groups, own, far, partial, partial_sib, turned, scales):
    toks, width = own.shape[1:]
    cols, both = partial.shape
    scale_keys, scale_back = scales
    pieces = [k for group in groups for k in group]
    n = len(pieces)
    held_far, part = parts_of(pieces, far)
    p = len(held_far)

    def body(own_ref, *refs):
        far_refs, (p_ref, q_ref, t_ref, k_ref), refs = refs[:p], refs[p : p + 4], refs[p + 4 :]
        for here, there in ((slice(0, toks), slice(toks, both)), (slice(toks, both), slice(0, toks))):
            value = (p_ref[:, here] + q_ref[:, there].astype(f32)) * scale_keys - t_ref[:, here]
            k_ref[:, here] = (value * scale_back).astype(bf16)
        for o_ref, group in zip(refs, groups):
            for slab, k in enumerate(group):
                value = jnp.dot(k_ref[:, :toks], own_ref[k], preferred_element_type=f32)
                block = far_refs[part[k]][k % PART]
                value += jnp.dot(k_ref[:, toks:], block, preferred_element_type=f32)
                o_ref[slab] = value.astype(bf16)

    return pl.pallas_call(
        body,
        in_specs=in_vmem(4 + p),
        out_specs=in_vmem(1 + len(groups)),
        out_shape=[jax.ShapeDtypeStruct((cols, both), bf16)]
        + [jax.ShapeDtypeStruct((len(group), cols, width), bf16) for group in groups],
        compiler_params=params(),
        cost_estimate=cost(4 * n * toks * cols * width, cols * toks * 28),
    )(own, *held_far, partial, partial_sib, turned)


def combine(rows, kind, *values):
    shape = values[0].shape[-2:]

    def body(*refs):
        def term(i, slab):
            ref = refs[i]
            return (ref[...] if len(ref.shape) == 2 else ref[slab]).astype(f32)

        for slab, terms in enumerate(rows):
            value = term(*terms[0])
            for extra in terms[1:]:
                value = value + term(*extra)
            refs[-1][slab] = value.astype(kind)

    return pl.pallas_call(
        body,
        in_specs=in_vmem(len(values)),
        out_specs=pl.BlockSpec(memory_space=VM),
        out_shape=jax.ShapeDtypeStruct((len(rows),) + shape, kind),
        compiler_params=params(),
        cost_estimate=cost(0, len(rows) * shape[0] * shape[1] * 8),
    )(*values)


def fragment_delta(fragment, outer, weight):
    rows, width = outer.shape
    cols = width // FRAGS

    def body(g_ref, o_ref, w_ref, d_ref):
        for q in range(FRAGS):
            at = slice(q * cols, (q + 1) * cols)

            @pl.when(g_ref[0] == q)
            def _():
                d_ref[...] = o_ref[:, at] - w_ref[:, at]

    return pl.pallas_call(
        body,
        in_specs=[SCALARS] + in_vmem(2),
        out_specs=pl.BlockSpec(memory_space=VM),
        out_shape=jax.ShapeDtypeStruct((rows, cols), f32),
        compiler_params=params(),
        cost_estimate=cost(0, rows * cols * 12),
    )(fragment, outer, weight)


def outer_step(fragment, summed, outer, moment, replicas):
    rows, width = outer.shape
    cols = width // FRAGS

    def body(g_ref, d_ref, o_ref, m_ref, oo_ref, mo_ref):
        mean = d_ref[...] / replicas
        for q in range(FRAGS):
            at = slice(q * cols, (q + 1) * cols)
            here = g_ref[0] == q
            old, mom = o_ref[:, at], m_ref[:, at]
            mom_new = 0.9 * mom + mean
            mo_ref[:, at] = jnp.where(here, mom_new, mom)
            oo_ref[:, at] = jnp.where(here, old - 0.7 * (mean + 0.9 * mom_new), old)

    return pl.pallas_call(
        body,
        in_specs=[SCALARS] + in_vmem(3),
        out_specs=in_vmem(2),
        out_shape=[jax.ShapeDtypeStruct((rows, width), f32)] * 2,
        compiler_params=params(),
        cost_estimate=cost(0, rows * width * 16),
    )(fragment, summed, outer, moment)


def inner_step(fragment, parts, weight, first, second, outer_out):
    rows, width = weight.shape
    cols = width // FRAGS

    def body(g_ref, p0, p1, p2, w_ref, f_ref, s_ref, o_ref, inner, fo_ref, so_ref):
        for q in range(FRAGS):
            at = slice(q * cols, (q + 1) * cols)
            turned = p0[0, at, :] + p1[0, at, :].astype(f32) + p2[1, at, :].astype(f32)
            grad = turned.T
            fn = 0.9 * f_ref[:, at] + 0.1 * grad
            sn = 0.95 * s_ref[:, at] + 0.05 * grad * grad
            update = fn / first_fix / (jnp.sqrt(sn / second_fix) + 1e-08)
            w = w_ref[:, at]
            stepped = w - 0.02 * (update + 0.1 * w)
            fo_ref[:, at] = fn
            so_ref[:, at] = sn
            inner[:, at] = jnp.where(g_ref[0] == q, 0.5 * stepped + 0.5 * o_ref[:, at], stepped)

    return pl.pallas_call(
        body,
        in_specs=[SCALARS] + in_vmem(7),
        out_specs=in_vmem(3),
        out_shape=[jax.ShapeDtypeStruct((rows, width), f32)] * 3,
        compiler_params=params(),
        cost_estimate=cost(0, rows * width * 38),
    )(fragment, *parts, weight, first, second, outer_out)


def shards(
    acts,
    doc_ids,
    target,
    inner_weight,
    adam_first,
    adam_second,
    outer_weight,
    outer_moment,
    fragment,
):
    tok_count = acts.shape[1]
    group_tokens = tok_count * lax.axis_size("fsdp")
    features = acts[0]
    weight = inner_weight[0]
    width = weight.shape[0]
    me = lax.axis_index("fsdp")
    c, z, x = me % 2, (me // 2) % NZ, me // (2 * NZ)

    def column_blocks(core):
        s = way(core)

        def at(dx, dz, other):
            half = 1 - core if other else core
            return ((x + dx) % NX * NZ + (z + dz) % NZ) * 2 + half

        order = [at(0, 0, 0), at(s, 0, 0), at(s, 0, 1), at(2, 0, 0)]
        order += [at(0, s, 0), at(0, s, 1), at(s, s, 0), at(s, s, 1), at(2, s, 0)]
        order += [at(s, -s, 0), at(s, -s, 1), at(2, -s, 0)]
        order += [at(0, 2, 0), at(s, 2, 0), at(s, 2, 1), at(2, 2, 0)]
        return jnp.stack(order).astype(jnp.int32)

    blocks, blocks_sib = column_blocks(c), column_blocks(1 - c)

    base = jnp.stack([me, me ^ 1]).astype(jnp.int32) * tok_count

    replicas = lax.axis_size("replica")
    summed = fragment_delta(fragment, outer_weight, weight)

    def swapped(value, step):
        return value + lax.ppermute(value, "replica", [(r, r ^ step) for r in range(replicas)])

    def pair(first, i, second, j):
        return combine([[(0, i)], [(1, j)]], bf16, first, second)

    def together(*values):
        return lax.optimization_barrier(values)

    a0 = turn_weight(weight, doc_ids, base)
    b0 = move(a0, SIBLING)
    S0 = pair(a0, 0, b0, 0)
    X0 = move(S0, FROM_X)
    Z1 = move(S0, FROM_Z)
    own, share = pick_columns(features, after(blocks, S0), blocks_sib, width)
    F0 = move(after(X0[0], own), FROM_X)
    X0, Z1, F0, own, summed, *share = together(X0, Z1, F0, own, summed, *share)

    C1 = move(Z1, SIBLING)
    X1 = move(Z1, FROM_X)
    a2 = move(Z1[0], FROM_Z)
    X2 = move(C1, FROM_X)
    far0 = move(after(share[0], C1), SIBLING)
    far1 = move(after(share[1], C1), SIBLING)
    b2 = move(after(a2, X1), SIBLING)
    X1, X2, a2, b2, far0, far1, *share = together(X1, X2, a2, b2, far0, far1, *share)

    F12 = move(pair(X1, 0, X2, 1), FROM_X)
    S3 = pair(a2, 0, b2, 0)
    X3 = move(S3, FROM_X)
    far2 = move(share[2], SIBLING)
    far3 = move(share[3], SIBLING)
    ids_sib = move(after(doc_ids, b2), SIBLING)
    target_sib = move(after(target[0], b2), SIBLING)
    far = (far0, far1, far2, far3)
    keys = add_keys([(0,), (1, 2), (3,)], own, far, (a0, X0, F0), None)
    keys = add_keys([(4, 5), (6, 7), (10, 9)], own, far, (Z1, X1, X2), keys)
    summed = swapped(after(summed, b2), 4)
    X3, F12, keys, ids_sib, target_sib, summed = together(
        X3, F12, keys, ids_sib, target_sib, summed
    )

    F2 = move(X3[0], FROM_X)
    keys = add_keys([(12,), (13, 14), (8, 11)], own, far, (a2, X3, F12), keys)
    F2, keys = together(F2, keys)
    notes = read_notes(a0, X0, F0, Z1, X1, X2, a2, X3, F12, F2)
    notes_sib = move(notes, SIBLING)
    partial, rounded = add_keys([(15,)], own, far, (after(F2, notes),), keys, send=True)
    partial_sib = move(after(rounded, notes_sib), SIBLING)

    index = jnp.arange(HEAD // 2, dtype=f32)
    freqs = jnp.exp(index * f32(-2.0 * math.log(theta_base) / HEAD))[:, None]
    angles = token_angles(base, notes, notes_sib, doc_ids, ids_sib, freqs)
    turned = turn_target(target[0], target_sib, jnp.cos(angles), jnp.sin(angles))
    scales = (D ** (-0.5), group_tokens ** (-0.5))
    back, PF2 = first_grads(((15,),), own, far, partial, partial_sib, turned, scales)

    f2 = move(PF2, TO_X)
    PF1, P2 = grads([((8, 11), bf16), ((12, 13, 14), f32)], own, far, back)
    f1 = move(PF1, TO_X)
    summed = swapped(after(summed, back), 1)
    s2 = combine([[(0, 1), (1, 0)], [(0, 2)]], bf16, P2, f2)
    g2 = move(s2, TO_X)
    PM, PN = grads([((9, 10), f32), ((4, 5, 6, 7), f32)], own, far, after(back, s2))
    f1 = after(f1, PN, summed)
    s1 = combine([[(1, 3)], [(0, 0), (2, 1)], [(1, 2), (2, 0)], [(0, 1)]], bf16, PM, PN, f1)
    g1 = move(s1, TO_X)
    P0, PF0 = grads([((0, 1, 2), f32), ((3,), bf16)], own, far, after(back, s1))
    f0 = move(PF0, TO_X)
    g2, s1 = together(g2, s1)
    s3 = combine([[(0, 0), (1, 0), (2, 1)]], bf16, P2, g2, move(g2, SIBLING))
    u2 = move(s3, TO_Z)
    summed = swapped(after(summed, s3), 2)
    g1, u2, f0, summed = together(g1, u2, f0, summed)
    c1 = move(g1, SIBLING)
    s4 = combine(
        [[(0, 0), (1, 2), (2, 3), (3, 0)], [(0, 1), (1, 0), (2, 1)]], bf16, PN, g1, c1, u2
    )
    h = move(s4, TO_Z)
    s0 = combine([[(0, 1), (1, 0)], [(0, 2)]], bf16, P0, after(f0, s4))
    g0 = move(s0, TO_X)
    outer_out, moment_out = outer_step(
        fragment, after(summed, s0), outer_weight, outer_moment, replicas
    )
    g0, h = together(g0, h)
    mine = combine([[(0, 0), (1, 0), (2, 1)]], f32, P0, g0, move(g0, SIBLING))
    inner_out, first_out, second_out = inner_step(
        fragment, (mine, h, move(h, SIBLING)), weight, adam_first[0], adam_second[0], outer_out
    )
    return (inner_out[None], first_out[None], second_out[None], outer_out, moment_out)


def solution(mesh):
    in_specs = (
        P("replica", "fsdp", None),
        P("replica", "fsdp"),
        P("replica", "fsdp", None),
        P("replica", "fsdp", None),
        P("replica", "fsdp", None),
        P("replica", "fsdp", None),
        P("fsdp", None),
        P("fsdp", None),
        P(),
    )
    out_specs = (
        P("replica", "fsdp", None),
        P("replica", "fsdp", None),
        P("replica", "fsdp", None),
        P("fsdp", None),
        P("fsdp", None),
    )
    return jax.shard_map(shards, mesh=mesh, in_specs=in_specs, out_specs=out_specs, check_vma=False)
```

```python
import math

import jax
import jax.numpy as jnp
from jax import lax
from jax.experimental import pallas as pl
from jax.experimental.pallas import tpu as pltpu
from jax.sharding import PartitionSpec as P

D = 8192
HEAD = 128
FRAGS = 4
DOCS = 8

theta_base = 500000.0
first_fix = 0.9999734386011124
second_fix = 0.9940794707796672

f32 = jnp.float32
bf16 = jnp.bfloat16
VM = pltpu.VMEM
LIMIT = 16 * 1024 * 1024
NOTE = 16
NOWHERE = 128 * 255
NT = (((1,), (1,)), ((), ()))
SCALARS = pl.BlockSpec(memory_space=pltpu.SMEM)

NX, NZ = 4, 4
TORUS = [(x, z, c) for x in range(NX) for z in range(NZ) for c in range(2)]


def place(x, z, c):
    return ((x % NX) * NZ + z % NZ) * 2 + c


def pairs(target):
    return [(place(*at), place(*target(*at))) for at in TORUS]


def way(c):
    return 1 - 2 * c


FROM_X = pairs(lambda x, z, c: (x - way(c), z, c))
FROM_Z = pairs(lambda x, z, c: (x, z - way(c), c))
TO_X = pairs(lambda x, z, c: (x + way(c), z, c))
TO_Z = pairs(lambda x, z, c: (x, z + way(c), c))
SIBLING = pairs(lambda x, z, c: (x, z, 1 - c))


def move(value, table):
    return lax.ppermute(value, "fsdp", table)


def after(value, *others):
    return lax.optimization_barrier((value,) + others)[0]


def params(limit=LIMIT):
    return pltpu.CompilerParams(vmem_limit_bytes=limit)


def cost(flops, moved):
    return pl.CostEstimate(flops=flops, bytes_accessed=moved, transcendentals=0)


def in_vmem(n):
    return [pl.BlockSpec(memory_space=VM)] * n


def turn_weight(weight, ids, first):
    rows, cols = weight.shape
    toks = ids.shape[1]

    def body(f_ref, w_ref, i_ref, o_ref):
        o_ref[:cols, :] = w_ref[...].T.astype(bf16)
        number = lax.broadcasted_iota(jnp.int32, (DOCS, toks), 0)
        token = lax.broadcasted_iota(jnp.int32, (DOCS, toks), 1) + f_ref[0]
        found = jnp.where(i_ref[...] == number, token, NOWHERE).astype(f32)
        start = jnp.min(found, axis=1, keepdims=True)
        high = jnp.floor(start * (1.0 / 128.0))
        low = start - 128.0 * high
        digits = jnp.concatenate([high, low], axis=0)
        o_ref[cols:, :] = jnp.broadcast_to(digits, (NOTE, rows)).astype(bf16)

    return pl.pallas_call(
        body,
        in_specs=[SCALARS] + in_vmem(2),
        out_specs=pl.BlockSpec(memory_space=VM),
        out_shape=jax.ShapeDtypeStruct((cols + NOTE, rows), bf16),
        compiler_params=params(),
        cost_estimate=cost(0, rows * cols * 6),
    )(first, weight, ids)


def read_notes(*values):
    rows, width = values[0].shape[-2:]
    cols = rows - NOTE

    def body(*refs):
        least = None
        for ref in refs[:-1]:
            if len(ref.shape) == 2:
                notes = [ref[cols:, :]]
            else:
                notes = [ref[i, cols:, :] for i in range(ref.shape[0])]
            for note in notes:
                digits = note.astype(f32)
                start = 128.0 * digits[:DOCS] + digits[DOCS:]
                least = start if least is None else jnp.minimum(least, start)
        refs[-1][...] = least

    return pl.pallas_call(
        body,
        in_specs=in_vmem(len(values)),
        out_specs=pl.BlockSpec(memory_space=VM),
        out_shape=jax.ShapeDtypeStruct((DOCS, width), f32),
        compiler_params=params(),
        cost_estimate=cost(0, len(values) * 100000),
    )(*values)


def token_angles(base, notes, notes_sib, ids, ids_sib, freqs):
    toks = ids.shape[1]
    half = freqs.shape[0]

    def body(b_ref, n_ref, m_ref, i_ref, j_ref, f_ref, o_ref):
        starts = jnp.minimum(n_ref[...], m_ref[...])[:, :1]
        number = lax.broadcasted_iota(jnp.int32, (DOCS, toks), 0)
        token = lax.broadcasted_iota(jnp.int32, (1, toks), 1)
        for k, ref in enumerate((i_ref, j_ref)):
            began = jnp.sum(jnp.where(ref[...] == number, starts, 0.0), axis=0, keepdims=True)
            position = (token + b_ref[k]).astype(f32) - began
            o_ref[:, k * toks : (k + 1) * toks] = f_ref[...] * position

    return pl.pallas_call(
        body,
        in_specs=[SCALARS] + in_vmem(5),
        out_specs=pl.BlockSpec(memory_space=VM),
        out_shape=jax.ShapeDtypeStruct((half, 2 * toks), f32),
        compiler_params=params(),
        cost_estimate=cost(0, half * toks * 16),
    )(base, notes, notes_sib, ids, ids_sib, freqs)


def turn_target(target, target_sib, cosine, sine):
    toks, cols = target.shape
    half = HEAD // 2

    def body(t_ref, u_ref, c_ref, s_ref, o_ref):
        for k, ref in enumerate((t_ref, u_ref)):
            here = slice(k * toks, (k + 1) * toks)
            cosv, sinv = c_ref[:, here], s_ref[:, here]
            for head in range(cols // HEAD):
                at = head * HEAD
                turned = ref[:, at : at + HEAD].astype(f32).T
                u, w = turned[:half], turned[half:]
                o_ref[at : at + half, here] = u * cosv + w * sinv
                o_ref[at + half : at + HEAD, here] = w * cosv - u * sinv

    return pl.pallas_call(
        body,
        in_specs=in_vmem(4),
        out_specs=pl.BlockSpec(memory_space=VM),
        out_shape=jax.ShapeDtypeStruct((cols, 2 * toks), f32),
        compiler_params=params(),
        cost_estimate=cost(0, toks * cols * 12),
    )(target, target_sib, cosine, sine)


PART = 4


def pick_columns(features, blocks, blocks_sib, width):
    toks, depth = features.shape
    count = blocks.shape[0]
    rows = toks // 8

    def body(b_ref, d_ref, f_ref, o_ref, *s_refs):
        for k in range(count):
            at = pl.multiple_of(d_ref[k] * width, width)
            s_refs[k // PART][k % PART] = f_ref[:, pl.ds(at, width)]
        for k in range(count):
            at = pl.multiple_of(b_ref[k] * width, width)
            o_ref[k] = f_ref[:, pl.ds(at, width)]

    def stack(n):
        return jax.ShapeDtypeStruct((n, toks, width), features.dtype)

    def spec(n):
        return pl.BlockSpec((n, rows, width), lambda i, b, d: (0, i, 0))

    parts = count // PART
    out = pl.pallas_call(
        body,
        grid_spec=pltpu.PrefetchScalarGridSpec(
            num_scalar_prefetch=2,
            grid=(toks // rows,),
            in_specs=[pl.BlockSpec((rows, depth), lambda i, b, d: (i, 0))],
            out_specs=[spec(count)] + [spec(PART)] * parts,
        ),
        out_shape=[stack(count)] + [stack(PART)] * parts,
        compiler_params=params(),
        cost_estimate=cost(0, toks * count * width * 8),
    )(blocks, blocks_sib, features)
    return out[0], out[1:]


def parts_of(pieces, far):
    used = sorted({k // PART for k in pieces})
    return [far[p] for p in used], {k: used.index(k // PART) for k in pieces}


def add_keys(pieces, own, far, weights, total, send=False):
    toks = own.shape[1]
    rows, width = weights[0].shape[-2:]
    cols = rows - NOTE
    m = len(weights)
    names = [k for held in pieces for k in held]
    n = len(names)
    held_far, part = parts_of(names, far)
    p = len(held_far)
    extra = [] if total is None else [total]

    def body(own_ref, *refs):
        far_refs, refs = refs[:p], refs[p:]
        o_ref = refs[m + len(extra)]
        values = [None, None]
        if total is not None:
            values = [refs[m][:, :toks], refs[m][:, toks:]]
        for w_ref, held in zip(refs, pieces):
            for slab, k in enumerate(held):
                w = w_ref[:cols, :] if len(w_ref.shape) == 2 else w_ref[slab, :cols, :]
                for j, block in enumerate((own_ref[k], far_refs[part[k]][k % PART])):
                    term = lax.dot_general(w, block, NT, preferred_element_type=f32)
                    values[j] = term if values[j] is None else values[j] + term
        o_ref[:, :toks] = values[0]
        o_ref[:, toks:] = values[1]
        if send:
            refs[-1][:, :toks] = values[0].astype(bf16)
            refs[-1][:, toks:] = values[1].astype(bf16)

    kinds = [f32, bf16] if send else [f32]
    out = pl.pallas_call(
        body,
        in_specs=in_vmem(1 + p + m + len(extra)),
        out_specs=in_vmem(len(kinds)),
        out_shape=[jax.ShapeDtypeStruct((cols, 2 * toks), kind) for kind in kinds],
        compiler_params=params(),
        cost_estimate=cost(4 * n * toks * cols * width, cols * toks * 8),
    )(own, *held_far, *weights, *extra)
    return out if send else out[0]


def grads(pieces, own, far, back):
    toks, width = own.shape[1:]
    cols = back.shape[0]
    names = [k for held, _ in pieces for k in held]
    n = len(names)
    held_far, part = parts_of(names, far)
    p = len(held_far)

    def body(own_ref, *refs):
        far_refs, k_ref, refs = refs[:p], refs[p], refs[p + 1 :]
        for o_ref, (held, kind) in zip(refs, pieces):
            for slab, k in enumerate(held):
                value = jnp.dot(k_ref[:, :toks], own_ref[k], preferred_element_type=f32)
                block = far_refs[part[k]][k % PART]
                value += jnp.dot(k_ref[:, toks:], block, preferred_element_type=f32)
                o_ref[slab] = value.astype(kind)

    return pl.pallas_call(
        body,
        in_specs=in_vmem(2 + p),
        out_specs=in_vmem(len(pieces)),
        out_shape=[jax.ShapeDtypeStruct((len(held), cols, width), kind) for held, kind in pieces],
        compiler_params=params(),
        cost_estimate=cost(4 * n * toks * cols * width, n * toks * width * 4),
    )(own, *held_far, back)


def first_grads(groups, own, far, partial, partial_sib, turned, scales):
    toks, width = own.shape[1:]
    cols, both = partial.shape
    scale_keys, scale_back = scales
    pieces = [k for group in groups for k in group]
    n = len(pieces)
    held_far, part = parts_of(pieces, far)
    p = len(held_far)

    def body(own_ref, *refs):
        far_refs, (p_ref, q_ref, t_ref, k_ref), refs = refs[:p], refs[p : p + 4], refs[p + 4 :]
        for here, there in ((slice(0, toks), slice(toks, both)), (slice(toks, both), slice(0, toks))):
            value = (p_ref[:, here] + q_ref[:, there].astype(f32)) * scale_keys - t_ref[:, here]
            k_ref[:, here] = (value * scale_back).astype(bf16)
        for o_ref, group in zip(refs, groups):
            for slab, k in enumerate(group):
                value = jnp.dot(k_ref[:, :toks], own_ref[k], preferred_element_type=f32)
                block = far_refs[part[k]][k % PART]
                value += jnp.dot(k_ref[:, toks:], block, preferred_element_type=f32)
                o_ref[slab] = value.astype(bf16)

    return pl.pallas_call(
        body,
        in_specs=in_vmem(4 + p),
        out_specs=in_vmem(1 + len(groups)),
        out_shape=[jax.ShapeDtypeStruct((cols, both), bf16)]
        + [jax.ShapeDtypeStruct((len(group), cols, width), bf16) for group in groups],
        compiler_params=params(),
        cost_estimate=cost(4 * n * toks * cols * width, cols * toks * 28),
    )(own, *held_far, partial, partial_sib, turned)


def combine(rows, kind, *values):
    shape = values[0].shape[-2:]

    def body(*refs):
        def term(i, slab):
            ref = refs[i]
            return (ref[...] if len(ref.shape) == 2 else ref[slab]).astype(f32)

        for slab, terms in enumerate(rows):
            value = term(*terms[0])
            for extra in terms[1:]:
                value = value + term(*extra)
            refs[-1][slab] = value.astype(kind)

    return pl.pallas_call(
        body,
        in_specs=in_vmem(len(values)),
        out_specs=pl.BlockSpec(memory_space=VM),
        out_shape=jax.ShapeDtypeStruct((len(rows),) + shape, kind),
        compiler_params=params(),
        cost_estimate=cost(0, len(rows) * shape[0] * shape[1] * 8),
    )(*values)


def fragment_delta(fragment, outer, weight):
    rows, width = outer.shape
    cols = width // FRAGS

    def body(g_ref, o_ref, w_ref, d_ref):
        for q in range(FRAGS):
            at = slice(q * cols, (q + 1) * cols)

            @pl.when(g_ref[0] == q)
            def _():
                d_ref[...] = o_ref[:, at] - w_ref[:, at]

    return pl.pallas_call(
        body,
        in_specs=[SCALARS] + in_vmem(2),
        out_specs=pl.BlockSpec(memory_space=VM),
        out_shape=jax.ShapeDtypeStruct((rows, cols), f32),
        compiler_params=params(),
        cost_estimate=cost(0, rows * cols * 12),
    )(fragment, outer, weight)


def outer_step(fragment, summed, outer, moment, replicas):
    rows, width = outer.shape
    cols = width // FRAGS

    def body(g_ref, d_ref, o_ref, m_ref, oo_ref, mo_ref):
        mean = d_ref[...] / replicas
        for q in range(FRAGS):
            at = slice(q * cols, (q + 1) * cols)
            here = g_ref[0] == q
            old, mom = o_ref[:, at], m_ref[:, at]
            mom_new = 0.9 * mom + mean
            mo_ref[:, at] = jnp.where(here, mom_new, mom)
            oo_ref[:, at] = jnp.where(here, old - 0.7 * (mean + 0.9 * mom_new), old)

    return pl.pallas_call(
        body,
        in_specs=[SCALARS] + in_vmem(3),
        out_specs=in_vmem(2),
        out_shape=[jax.ShapeDtypeStruct((rows, width), f32)] * 2,
        compiler_params=params(),
        cost_estimate=cost(0, rows * width * 16),
    )(fragment, summed, outer, moment)


def inner_step(fragment, parts, weight, first, second, outer_out):
    rows, width = weight.shape
    cols = width // FRAGS

    def body(g_ref, p0, p1, p2, w_ref, f_ref, s_ref, o_ref, inner, fo_ref, so_ref):
        for q in range(FRAGS):
            at = slice(q * cols, (q + 1) * cols)
            turned = p0[0, at, :] + p1[0, at, :].astype(f32) + p2[1, at, :].astype(f32)
            grad = turned.T
            fn = 0.9 * f_ref[:, at] + 0.1 * grad
            sn = 0.95 * s_ref[:, at] + 0.05 * grad * grad
            update = fn / first_fix / (jnp.sqrt(sn / second_fix) + 1e-08)
            w = w_ref[:, at]
            stepped = w - 0.02 * (update + 0.1 * w)
            fo_ref[:, at] = fn
            so_ref[:, at] = sn
            inner[:, at] = jnp.where(g_ref[0] == q, 0.5 * stepped + 0.5 * o_ref[:, at], stepped)

    return pl.pallas_call(
        body,
        in_specs=[SCALARS] + in_vmem(7),
        out_specs=in_vmem(3),
        out_shape=[jax.ShapeDtypeStruct((rows, width), f32)] * 3,
        compiler_params=params(),
        cost_estimate=cost(0, rows * width * 38),
    )(fragment, *parts, weight, first, second, outer_out)


def shards(
    acts,
    doc_ids,
    target,
    inner_weight,
    adam_first,
    adam_second,
    outer_weight,
    outer_moment,
    fragment,
):
    tok_count = acts.shape[1]
    group_tokens = tok_count * lax.axis_size("fsdp")
    features = acts[0]
    weight = inner_weight[0]
    width = weight.shape[0]
    me = lax.axis_index("fsdp")
    c, z, x = me % 2, (me // 2) % NZ, me // (2 * NZ)

    def column_blocks(core):
        s = way(core)

        def at(dx, dz, other):
            half = 1 - core if other else core
            return ((x + dx) % NX * NZ + (z + dz) % NZ) * 2 + half

        order = [at(0, 0, 0), at(s, 0, 0), at(s, 0, 1), at(2, 0, 0)]
        order += [at(0, s, 0), at(0, s, 1), at(s, s, 0), at(s, s, 1), at(2, s, 0)]
        order += [at(s, -s, 0), at(s, -s, 1), at(2, -s, 0)]
        order += [at(0, 2, 0), at(s, 2, 0), at(s, 2, 1), at(2, 2, 0)]
        return jnp.stack(order).astype(jnp.int32)

    blocks, blocks_sib = column_blocks(c), column_blocks(1 - c)

    base = jnp.stack([me, me ^ 1]).astype(jnp.int32) * tok_count

    replicas = lax.axis_size("replica")
    summed = fragment_delta(fragment, outer_weight, weight)

    def swapped(value, step):
        return value + lax.ppermute(value, "replica", [(r, r ^ step) for r in range(replicas)])

    def pair(first, i, second, j):
        return combine([[(0, i)], [(1, j)]], bf16, first, second)

    def together(*values):
        return lax.optimization_barrier(values)

    a0 = turn_weight(weight, doc_ids, base)
    b0 = move(a0, SIBLING)
    S0 = pair(a0, 0, b0, 0)
    X0 = move(S0, FROM_X)
    Z1 = move(S0, FROM_Z)
    own, share = pick_columns(features, after(blocks, S0), blocks_sib, width)
    F0 = move(after(X0[0], own), FROM_X)
    X0, Z1, F0, own, summed, *share = together(X0, Z1, F0, own, summed, *share)

    C1 = move(Z1, SIBLING)
    X1 = move(Z1, FROM_X)
    a2 = move(Z1[0], FROM_Z)
    X2 = move(C1, FROM_X)
    far0 = move(after(share[0], C1), SIBLING)
    far1 = move(after(share[1], C1), SIBLING)
    b2 = move(after(a2, X1), SIBLING)
    X1, X2, a2, b2, far0, far1, *share = together(X1, X2, a2, b2, far0, far1, *share)

    F12 = move(pair(X1, 0, X2, 1), FROM_X)
    S3 = pair(a2, 0, b2, 0)
    X3 = move(S3, FROM_X)
    far2 = move(share[2], SIBLING)
    far3 = move(share[3], SIBLING)
    ids_sib = move(after(doc_ids, b2), SIBLING)
    target_sib = move(after(target[0], b2), SIBLING)
    far = (far0, far1, far2, far3)
    keys = add_keys([(0,), (1, 2), (3,)], own, far, (a0, X0, F0), None)
    keys = add_keys([(4, 5), (6, 7), (10, 9)], own, far, (Z1, X1, X2), keys)
    summed = swapped(after(summed, b2), 4)
    X3, F12, keys, ids_sib, target_sib, summed = together(
        X3, F12, keys, ids_sib, target_sib, summed
    )

    F2 = move(X3[0], FROM_X)
    keys = add_keys([(12,), (13, 14), (8, 11)], own, far, (a2, X3, F12), keys)
    F2, keys = together(F2, keys)
    notes = read_notes(a0, X0, F0, Z1, X1, X2, a2, X3, F12, F2)
    notes_sib = move(notes, SIBLING)
    partial, rounded = add_keys([(15,)], own, far, (after(F2, notes),), keys, send=True)
    partial_sib = move(after(rounded, notes_sib), SIBLING)

    index = jnp.arange(HEAD // 2, dtype=f32)
    freqs = jnp.exp(index * f32(-2.0 * math.log(theta_base) / HEAD))[:, None]
    angles = token_angles(base, notes, notes_sib, doc_ids, ids_sib, freqs)
    turned = turn_target(target[0], target_sib, jnp.cos(angles), jnp.sin(angles))
    scales = (D ** (-0.5), group_tokens ** (-0.5))
    back, PF2 = first_grads(((15,),), own, far, partial, partial_sib, turned, scales)

    f2 = move(PF2, TO_X)
    PF1, P2 = grads([((8, 11), bf16), ((12, 13, 14), f32)], own, far, back)
    f1 = move(PF1, TO_X)
    summed = swapped(after(summed, back), 1)
    s2 = combine([[(0, 1), (1, 0)], [(0, 2)]], bf16, P2, f2)
    g2 = move(s2, TO_X)
    PM, PN = grads([((9, 10), f32), ((4, 5, 6, 7), f32)], own, far, after(back, s2))
    f1 = after(f1, PN, summed)
    s1 = combine([[(1, 3)], [(0, 0), (2, 1)], [(1, 2), (2, 0)], [(0, 1)]], bf16, PM, PN, f1)
    g1 = move(s1, TO_X)
    P0, PF0 = grads([((0, 1, 2), f32), ((3,), bf16)], own, far, after(back, s1))
    f0 = move(PF0, TO_X)
    g2, s1 = together(g2, s1)
    s3 = combine([[(0, 0), (1, 0), (2, 1)]], bf16, P2, g2, move(g2, SIBLING))
    u2 = move(s3, TO_Z)
    g1, u2, f0 = together(g1, u2, f0)
    c1 = move(g1, SIBLING)
    s4 = combine(
        [[(0, 0), (1, 2), (2, 3), (3, 0)], [(0, 1), (1, 0), (2, 1)]], bf16, PN, g1, c1, u2
    )
    h = move(s4, TO_Z)
    s0 = combine([[(0, 1), (1, 0)], [(0, 2)]], bf16, P0, after(f0, s4))
    g0 = move(s0, TO_X)
    summed = swapped(after(summed, s0), 2)
    outer_out, moment_out = outer_step(fragment, summed, outer_weight, outer_moment, replicas)
    g0, h, outer_out, moment_out = together(g0, h, outer_out, moment_out)
    mine = combine([[(0, 0), (1, 0), (2, 1)]], f32, P0, g0, move(g0, SIBLING))
    inner_out, first_out, second_out = inner_step(
        fragment, (mine, h, move(h, SIBLING)), weight, adam_first[0], adam_second[0], outer_out
    )
    return (inner_out[None], first_out[None], second_out[None], outer_out, moment_out)


def solution(mesh):
    in_specs = (
        P("replica", "fsdp", None),
        P("replica", "fsdp"),
        P("replica", "fsdp", None),
        P("replica", "fsdp", None),
        P("replica", "fsdp", None),
        P("replica", "fsdp", None),
        P("fsdp", None),
        P("fsdp", None),
        P(),
    )
    out_specs = (
        P("replica", "fsdp", None),
        P("replica", "fsdp", None),
        P("replica", "fsdp", None),
        P("fsdp", None),
        P("fsdp", None),
    )
    return jax.shard_map(shards, mesh=mesh, in_specs=in_specs, out_specs=out_specs, check_vma=False)
```
